32 devices in a mesh: parts: 2 (over x), cols: 16 (over z, y, core).
Axes of the slice: x: 2, y: 2, z: 4, core: 2. Of those that a mesh axis runs over, the one named last changes fastest.
Arguments:
- activations: bfloat16 [4096, 14336], P('parts', 'cols'), parts along dimension 0
- out_grads: bfloat16 [4096, 4096], P(('parts', 'cols')), parts along dimension 0
- queries: bfloat16 [4, 14336, 4096], P('parts', 'cols'), parts along dimension 0
- lengths: int32 [4], P('parts'), parts along dimension 0, may hold values from 256 to 1024, as said below
Outputs:
- influence: float32 [2, 4096], P(None, ('parts', 'cols')), parts along dimension 1
The draws below stay inside these ranges and needn't reach their ends.
There are 2 independent parts, one for each index of `parts`. The reference program is written for one: setup_inputs(seed, part) draws one part's arguments, and reference() takes and returns one part's arrays. A program takes and returns all parts, laid end to end along the dimension named above; each array names one. Nothing has to cross between parts.
Inputs may be any that keep to these rules, and one draw needn't show every extreme that they name: `lengths`: at least one sequence has the full length 1024.
All inputs are finite; a program needn't handle non-finite values.
Results may differ from the reference program's by a relative error of at most 0.0003.
Values may be sent and summed in bfloat16 or wider, within the bound.
A program may use at most 128 MiB of HBM per device.

```python
import math
import jax
import jax.numpy as jnp
from jax import lax

D = 4096
FF = 14336
NQ = 2
LEN = 1024
TOKENS = 2048
SEQS = 2


def rising_scales(key, count, share):
    offsets = jax.random.uniform(key, (count,), jnp.float32)
    places = jnp.arange(count, dtype=jnp.float32) / count
    return 10.0 ** (share * places + (1.0 - share) * offsets)


def draw_activations(key, part):
    key = jax.random.fold_in(key, 11)
    key_noise, key_cols, key_rows = jax.random.split(key, 3)
    noise = jax.random.normal(key_noise, (TOKENS, FF), jnp.float32)
    columns = rising_scales(key_cols, FF, 0.5)
    row_scales = 10.0 ** jax.random.uniform(key_rows, (TOKENS, 1), jnp.float32)
    return (0.2 * noise * columns[None, :] * row_scales).astype(jnp.bfloat16)


def draw_out_grads(key, part):
    key = jax.random.fold_in(key, 23)
    key_noise, key_cols, key_rows = jax.random.split(key, 3)
    noise = jax.random.normal(key_noise, (TOKENS, D), jnp.float32)
    columns = 10.0 ** jax.random.uniform(key_cols, (1, D), jnp.float32)
    row_scales = 10.0 ** jax.random.uniform(key_rows, (TOKENS, 1), jnp.float32)
    return (0.2 * noise * columns * row_scales).astype(jnp.bfloat16)


def draw_queries(key, part):
    key = jax.random.fold_in(key, 37)
    key_noise, key_rows, key_cols, key_each = jax.random.split(key, 4)
    noise = jax.random.normal(key_noise, (NQ, FF, D), jnp.float32)
    hidden_rows = rising_scales(key_rows, FF, 0.5)
    columns = 10.0 ** jax.random.uniform(key_cols, (1, 1, D), jnp.float32)
    per_query = 10.0 ** jax.random.uniform(key_each, (NQ, 1, 1), jnp.float32)
    return (0.05 * noise * hidden_rows[None, :, None] * columns * per_query).astype(jnp.bfloat16)


def draw_lengths(key, part):
    key = jax.random.fold_in(key, 41)
    key_len, key_full = jax.random.split(key)
    drawn = jax.random.randint(key_len, (SEQS,), LEN // 4, LEN + 1, jnp.int32)
    full_index = jax.random.randint(key_full, (), 0, SEQS, jnp.int32)
    return drawn.at[full_index].set(LEN)


def setup_inputs(seed: int = 0, part: int = 0) -> dict:
    keys = jax.random.split(jax.random.key(seed), 5)
    part_splits = jax.random.split(jax.random.fold_in(keys[4], part), 5)
    activations = draw_activations(jax.random.fold_in(jax.random.fold_in(keys[4], part), 71), part)
    out_grads = draw_out_grads(jax.random.fold_in(jax.random.fold_in(keys[4], part), 71), part)
    queries = draw_queries(jax.random.fold_in(jax.random.fold_in(keys[4], part), 71), part)
    lengths = draw_lengths(jax.random.fold_in(jax.random.fold_in(keys[4], part), 71), part)
    return {"activations": activations, "out_grads": out_grads, "queries": queries, "lengths": lengths}


epsilon = 1e-06

def reference(activations, out_grads, queries, lengths):
    act_float = activations.astype(jnp.float32)

    def one_query(query):
        projected = jnp.dot(out_grads, query.T, preferred_element_type=jnp.float32)
        return lax.optimization_barrier(jnp.sum(projected * act_float, axis=1))
    raw_scores = lax.map(one_query, queries)
    query_rms = jnp.sqrt(lax.optimization_barrier(jnp.sum(jnp.square(queries.astype(jnp.float32)), axis=(1, 2))) / (FF * D) + epsilon)
    act_rms = jnp.sqrt(lax.optimization_barrier(jnp.sum(jnp.square(act_float), axis=1)) / FF + epsilon)
    grad_rms = jnp.sqrt(lax.optimization_barrier(jnp.sum(jnp.square(out_grads.astype(jnp.float32)), axis=1)) / D + epsilon)
    positions = jnp.arange(TOKENS, dtype=jnp.int32)
    seq_limit = lengths[positions // LEN]
    keep_mask = positions % LEN < seq_limit
    denominator = query_rms[:, None] * act_rms[None, :] * grad_rms[None, :] * math.sqrt(FF * D)
    return jnp.where(keep_mask[None, :], raw_scores / denominator, jnp.float32(0.0))
```

```python
import functools
import math

import jax
import jax.numpy as jnp
from jax import lax
from jax.experimental import pallas as pl
from jax.experimental.pallas import tpu as pltpu
from jax.sharding import PartitionSpec as P

LEN = 1024
SUBS = 4
LANES = 128
MESH = pl.DeviceIdType.MESH

epsilon = 1e-06


def kernel(sizes, og, act, qry, lens, out, G, A, Q, acc, qtile, gsq, res, parts,
           recv, s_in, s_out, s_y, s_sib, r_send, r_recv, lsem):
    ncols, ff, d_model, seqs = sizes
    sub_rows = og.shape[1]
    half_rows = 2 * sub_rows
    tok = SUBS * sub_rows
    me = lax.axis_index("cols")
    z, y, c = lax.div(me, 4), lax.rem(lax.div(me, 2), 2), lax.rem(me, 2)
    hi = lax.div(z, 2)
    d = 1 - 2 * hi
    m = lax.rem(z + hi, 2)
    edge, mid = m == 0, m == 1
    own = 2 * z + y

    def dev(zz, yy, cc):
        return 4 * zz + 2 * yy + cc

    sib, ydev = dev(z, y, 1 - c), dev(z, 1 - y, c)
    indev, outdev = dev(z + d, y, c), dev(z - d, y, c)

    def copy(src, p, s, target, sem):
        return pltpu.make_async_remote_copy(
            src_ref=src, dst_ref=G.at[p, c, s], send_sem=sem, recv_sem=recv.at[2 * p + c, s],
            device_id={"cols": target}, device_id_type=MESH)

    def await_chunk(p, cc, s):
        pltpu.make_async_remote_copy(
            src_ref=G.at[p, cc, s], dst_ref=G.at[p, cc, s], send_sem=s_sib.at[0, 0],
            recv_sem=recv.at[2 * p + cc, s], device_id={"cols": sib}, device_id_type=MESH).wait_recv()

    loads = [pltpu.make_async_copy(og, G.at[own, c], lsem.at[0]),
             pltpu.make_async_copy(qry.at[0], Q.at[0], lsem.at[1]),
             pltpu.make_async_copy(qry.at[1], Q.at[1], lsem.at[2]),
             pltpu.make_async_copy(act, A, lsem.at[3])]
    for load in loads:
        load.start()

    barrier = pltpu.get_barrier_semaphore()

    def greet(k, _):
        pl.semaphore_signal(barrier, inc=1, device_id={"cols": lax.rem(me + k, ncols)}, device_id_type=MESH)
        return 0

    lax.fori_loop(1, ncols, greet, 0)
    pl.semaphore_wait(barrier, ncols - 1)

    for s in range(SUBS):
        copy(og.at[s], own, s, ydev, s_y.at[s]).start()
        copy(og.at[s], own, s, indev, s_in.at[s]).start()

        @pl.when(mid)
        def _():
            copy(og.at[s], own, s, outdev, s_out.at[s]).start()

        copy(og.at[s], own, s, sib, s_sib.at[own, s]).start()

    for load in loads:
        load.wait()

    row = lax.broadcasted_iota(jnp.int32, (8, LANES), 0)
    qbase = jnp.zeros((8, LANES), jnp.float32)
    for q in range(2):
        def add_squares(r, total):
            x = Q[q, pl.ds(pl.multiple_of(r * 16, 16), 16), :].astype(jnp.float32)
            x = x * x
            parts_ = [x[:, k * LANES:(k + 1) * LANES] for k in range(d_model // LANES)]
            while len(parts_) > 1:
                parts_ = [a + b for a, b in zip(parts_[::2], parts_[1::2])]
            return total + parts_[0]

        total = lax.fori_loop(0, Q.shape[1] // 16, add_squares, jnp.zeros((16, LANES), jnp.float32))
        qbase = jnp.where(row == 3 + q, jnp.sum(total), qbase)
    qtile[...] = qbase
    for s in range(SUBS):
        x = jnp.zeros((sub_rows, LANES), jnp.float32)
        for k in range(d_model // LANES):
            g = G[own, c, s, :, pl.ds(k * LANES, LANES)].astype(jnp.float32)
            x = x + g * g
        gsq[s * sub_rows:(s + 1) * sub_rows, :] = x

    def send_result(p, h, tile):
        res[2 * p + h] = tile
        for cc in range(2):
            target = 2 * p + cc

            @pl.when(target == me)
            def _():
                parts[me, h] = tile

            @pl.when(target != me)
            def _():
                pltpu.make_async_remote_copy(
                    src_ref=res.at[2 * p + h], dst_ref=parts.at[me, h], send_sem=r_send.at[2 * p + h, cc],
                    recv_sem=r_recv.at[me, h], device_id={"cols": target}, device_id_type=MESH).start()

    def compute(pa, ha, pb, hb):
        for p, h in ((pa, ha), (pb, hb)):
            for s in range(2):
                await_chunk(p, 1 - c, 2 * h + s)
        acc[...] = jnp.zeros_like(acc)

        def tile_step(i, _):
            cols = pl.ds(pl.multiple_of(i * LANES, LANES), LANES)
            lhs = jnp.concatenate([
                G[pa, :, pl.ds(2 * ha, 2)].reshape(2 * half_rows, d_model),
                G[pb, :, pl.ds(2 * hb, 2)].reshape(2 * half_rows, d_model)], axis=0)
            rhs = Q[:, cols, :].reshape(2 * LANES, d_model)
            pr = lax.dot_general(lhs, rhs, (((1,), (1,)), ((), ())), preferred_element_type=jnp.float32)
            a = jnp.concatenate([
                A[pa, :, pl.ds(2 * ha, 2), :, cols].reshape(2 * half_rows, LANES),
                A[pb, :, pl.ds(2 * hb, 2), :, cols].reshape(2 * half_rows, LANES)], axis=0).astype(jnp.float32)
            acc[0] += pr[:, :LANES] * a
            acc[1] += pr[:, LANES:] * a
            acc[2] += a * a
            return 0

        lax.fori_loop(0, Q.shape[1] // LANES, tile_step, 0)
        for j, (p, h) in enumerate(((pa, ha), (pb, hb))):
            tile = qtile[...]
            for k in range(3):
                block = acc[k, j * 2 * half_rows:(j + 1) * 2 * half_rows, :]
                tile = jnp.where(row == k, jnp.sum(block.T, axis=0, keepdims=True), tile)
            send_result(p, h, tile)

    z1, z2, z3, zo = z + d, z + 2 * d, z + 3 * d, z - d
    other = 1 - y

    def pick(a, b):
        return jnp.where(edge, a, b)

    def step(u, _):
        is_unit = functools.reduce(jnp.logical_or, [u == t for t in UNIT_STEPS])
        unit = sum([(u >= t).astype(jnp.int32) for t in UNIT_STEPS]) - 1

        @pl.when(is_unit)
        def _():
            pa, pb = own, own
            split = jnp.logical_and(edge, unit >= 6)
            table = (
                (own, own),
                (2 * z1 + y,) * 2,
                (2 * z + other,) * 2,
                (pick(2 * z2 + y, 2 * zo + y),) * 2,
                (pick(2 * z2 + other, 2 * zo + other),) * 2,
                (pick(2 * z3 + y, 2 * z2 + y),) * 2,
                (2 * z1 + other, pick(2 * z3 + other, 2 * z1 + other)),
                (pick(2 * z1 + other, 2 * z2 + other), pick(2 * z3 + other, 2 * z2 + other)),
            )
            for t, (a, b) in enumerate(table):
                pa = jnp.where(unit == t, a, pa)
                pb = jnp.where(unit == t, b, pb)
            ha = jnp.where(split, unit - 6, 0)
            hb = jnp.where(split, unit - 6, 1)
            compute(pa, ha, pb, hb)

        @pl.when(jnp.logical_and(u < 14, jnp.logical_or(edge, u < 8)))
        def _():
            own_line = u < 12
            p = jnp.where(own_line, 2 * (z + d * (1 + lax.div(u, 4))) + y, 2 * z1 + other)
            s = jnp.where(own_line, lax.rem(u, 4), u - 10)
            await_chunk(p, c, s)

            @pl.when(mid)
            def _():
                copy(G.at[p, c, s], p, s, outdev, s_out.at[4 + u]).start()

            skip = jnp.logical_and(edge, jnp.logical_or(jnp.logical_or(u == 2, u == 3), u >= 12))

            @pl.when(jnp.logical_not(skip))
            def _():
                k = pick(jnp.where(u < 2, 4 + u, u + 2), jnp.where(u < 2, 4 + 2 * u, u + 6))
                copy(G.at[p, c, s], p, s, ydev, s_y.at[k]).start()

            copy(G.at[p, c, s], p, s, sib, s_sib.at[p, s]).start()

        @pl.when(jnp.logical_and(mid, u < 6))
        def _():
            own_line = u < 4
            p = jnp.where(own_line, 2 * zo + y, 2 * zo + other)
            s = jnp.where(own_line, u, u - 2)
            await_chunk(p, c, s)

            @pl.when(own_line)
            def _():
                copy(G.at[p, c, s], p, s, indev, s_in.at[4 + u]).start()

            @pl.when(u < 2)
            def _():
                copy(G.at[p, c, s], p, s, ydev, s_y.at[5 + 2 * u]).start()

            copy(G.at[p, c, s], p, s, sib, s_sib.at[p, s]).start()

        @pl.when(u < 14)
        def _():
            ne = jnp.where(u < 6, u - 4, u - 2)
            ze, se = z + d * (1 + lax.div(ne, 4)), lax.rem(ne, 4)
            early = u < 8
            from_out = jnp.logical_and(early, lax.rem(u, 2) == 1)
            nm = jnp.where(early, lax.div(u - 4, 2), u - 6)
            zm, sm = jnp.where(from_out, zo, z + d * (1 + lax.div(nm, 4))), lax.rem(nm, 4)
            first = u < 4
            p = 2 * jnp.where(first, z, pick(ze, zm)) + other
            s = jnp.where(first, u, pick(se, sm))
            await_chunk(p, c, s)
            copy(G.at[p, c, s], p, s, sib, s_sib.at[p, s]).start()

            @pl.when(jnp.logical_and(edge, jnp.logical_or(u == 2, u == 3)))
            def _():
                copy(G.at[p, c, s], p, s, indev, s_in.at[2 + u]).start()

        @pl.when(jnp.logical_and(mid, jnp.logical_or(u == 8, u == 9)))
        def _():
            p, s = 2 * z + other, u - 6
            copy(G.at[p, c, s], p, s, outdev, s_out.at[4 + u]).start()

        return 0

    lax.fori_loop(0, 15, step, 0)

    def settle(sem):
        copy(og.at[0], own, 0, sib, sem).wait_send()

    def settle_y(k, _):
        settle(s_y.at[k])

        @pl.when(mid)
        def _():
            settle(s_out.at[k])

        @pl.when(k < pick(6, 8))
        def _():
            settle(s_in.at[k])

        return 0

    lax.fori_loop(0, 14, settle_y, 0)

    def settle_sib(p, _):
        for s in range(SUBS):
            settle(s_sib.at[p, s])
        return 0

    lax.fori_loop(0, ncols // 2, settle_sib, 0)

    def result(src, h, cc_sem):
        return pltpu.make_async_remote_copy(
            src_ref=res.at[0], dst_ref=parts.at[src, h], send_sem=cc_sem,
            recv_sem=r_recv.at[src, h], device_id={"cols": sib}, device_id_type=MESH)

    def gather_results(k, _):
        src = lax.rem(me + k, ncols)
        for h in range(2):
            result(src, h, r_send.at[0, 0]).wait_recv()
            p, cc = lax.div(src, 2), lax.rem(src, 2)
            result(src, h, r_send.at[2 * p + h, cc]).wait_send()
        return 0

    lax.fori_loop(1, ncols, gather_results, 0)

    t0, t1 = parts[0, 0], parts[0, 1]
    for src in range(1, ncols):
        t0, t1 = t0 + parts[src, 0], t1 + parts[src, 1]
    lane = lax.broadcasted_iota(jnp.int32, (1, LANES), 1)
    low = jnp.where(c == 0, t0, jnp.roll(t0, half_rows, axis=1))
    high = jnp.where(c == 0, jnp.roll(t1, half_rows, axis=1), t1)
    full = jnp.where(lane < half_rows, low, high)
    query_rms = jnp.sqrt(full[3:5] / (ff * d_model) + epsilon)
    act_rms = jnp.sqrt(full[2:3] / ff + epsilon)
    grad_rms = jnp.sqrt(jnp.sum(gsq[...].T, axis=0, keepdims=True) / d_model + epsilon)
    positions = me * tok + lane
    seq_ids = lax.div(positions, LEN)
    limit = jnp.zeros((1, LANES), jnp.int32)
    for q in range(seqs):
        limit = jnp.where(seq_ids == q, lens[q], limit)
    keep = lax.rem(positions, LEN) < limit
    influence = full[0:2] / (query_rms * act_rms * grad_rms * math.sqrt(ff * d_model))
    out[...] = jnp.where(keep, influence, 0.0)


UNIT_STEPS = (0, 4, 5, 8, 10, 12, 13, 14)


def fused(ncols, activations, out_grads, queries, lengths):
    tok, d_model = out_grads.shape
    nq, ff_dev, _ = queries.shape
    pairs, sub = ncols // 2, tok // SUBS
    sizes = (ncols, ff_dev * ncols, d_model, lengths.shape[0])
    tokens = ncols * tok
    dma = pltpu.SemaphoreType.DMA
    return pl.pallas_call(
        functools.partial(kernel, sizes),
        out_shape=jax.ShapeDtypeStruct((nq, tok), jnp.float32),
        in_specs=[pl.BlockSpec(memory_space=pl.ANY)] * 3 + [pl.BlockSpec(memory_space=pltpu.SMEM)],
        out_specs=pl.BlockSpec(memory_space=pltpu.VMEM),
        scratch_shapes=[
            pltpu.VMEM((pairs, 2, SUBS, sub, d_model), jnp.bfloat16),
            pltpu.VMEM((pairs, 2, SUBS, sub, ff_dev), jnp.bfloat16),
            pltpu.VMEM((nq, ff_dev, d_model), jnp.bfloat16),
            pltpu.VMEM((3, 2 * tok, LANES), jnp.float32),
            pltpu.VMEM((8, LANES), jnp.float32),
            pltpu.VMEM((tok, LANES), jnp.float32),
            pltpu.VMEM((2 * pairs, 8, LANES), jnp.float32),
            pltpu.VMEM((ncols, 2, 8, LANES), jnp.float32),
            dma((ncols, SUBS)), dma((8,)), dma((14,)), dma((14,)), dma((pairs, SUBS)),
            dma((2 * pairs, 2)), dma((ncols, 2)), dma((4,)),
        ],
        compiler_params=pltpu.CompilerParams(
            collective_id=0, has_side_effects=True, vmem_limit_bytes=54 * 2**20),
        cost_estimate=pl.CostEstimate(
            flops=2 * nq * tokens * ff_dev * d_model, transcendentals=0,
            bytes_accessed=2 * (nq * ff_dev * d_model + tokens * ff_dev + tok * d_model)),
    )(
        out_grads.reshape(SUBS, sub, d_model),
        activations.reshape(pairs, 2, SUBS, sub, ff_dev),
        queries, lengths)


def local(activations, out_grads, queries, lengths):
    tok_dev, d_model = out_grads.shape
    query_sq = jnp.sum(jnp.square(queries.astype(jnp.float32)), axis=(1, 2))
    gathered = lax.all_gather(out_grads, "cols", axis=0, tiled=True)
    projected = jnp.einsum("rd,qfd->qrf", gathered, queries, preferred_element_type=jnp.float32)
    partials = jnp.sum(projected * activations.astype(jnp.float32)[None], axis=2)
    act_sq = jnp.sum(jnp.square(activations.astype(jnp.float32)), axis=1)[None, :]
    own_first = lax.axis_index("cols") * tok_dev
    total_scores, total_act, query_total = lax.psum((partials, act_sq, query_sq), "cols")
    own_scores = lax.dynamic_slice_in_dim(total_scores, own_first, tok_dev, 1)
    own_act = lax.dynamic_slice_in_dim(total_act, own_first, tok_dev, 1)
    ff = queries.shape[1] * lax.axis_size("cols")
    query_rms = jnp.sqrt(query_total / (ff * d_model) + epsilon)
    act_rms = jnp.sqrt(own_act[0] / ff + epsilon)
    grad_rms = jnp.sqrt(jnp.sum(jnp.square(out_grads.astype(jnp.float32)), axis=1) / d_model + epsilon)
    positions = own_first + jnp.arange(tok_dev, dtype=jnp.int32)
    seq_ids = positions // LEN
    owner_match = seq_ids[:, None] == jnp.arange(lengths.shape[0], dtype=jnp.int32)[None, :]
    seq_limit = jnp.sum(jnp.where(owner_match, lengths[None, :], 0), axis=1)
    keep_mask = positions % LEN < seq_limit
    denominator = query_rms[:, None] * act_rms[None, :] * grad_rms[None, :] * math.sqrt(ff * d_model)
    return jnp.where(keep_mask[None, :], own_scores / denominator, jnp.float32(0.0))


def solution(mesh):
    in_specs = (
        P("parts", "cols"),
        P(("parts", "cols"), None),
        P("parts", "cols", None),
        P("parts"),
    )
    out_specs = P(None, ("parts", "cols"))
    ncols = mesh.shape["cols"]
    body = functools.partial(fused, ncols) if ncols == 16 else local
    return jax.shard_map(body, mesh=mesh, in_specs=in_specs, out_specs=out_specs, check_vma=False)
```

```python
import functools
import math

import jax
import jax.numpy as jnp
from jax import lax
from jax.experimental import pallas as pl
from jax.experimental.pallas import tpu as pltpu
from jax.sharding import PartitionSpec as P

LEN = 1024
SUBS = 4
LANES = 128
MESH = pl.DeviceIdType.MESH

epsilon = 1e-06


def kernel(sizes, og, act, qry, lens, out, G, A, AT, Q, acc, asq, qtile, gsq, res, parts,
           recv, s_in, s_out, s_y, s_sib, r_send, r_recv, lsem):
    ncols, ff, d_model, seqs = sizes
    tok = og.shape[0]
    width = d_model // SUBS
    ff_dev = Q.shape[1]
    pairs = ncols // 2
    me = lax.axis_index("cols")
    z, y, c = lax.div(me, 4), lax.rem(lax.div(me, 2), 2), lax.rem(me, 2)
    hi = lax.div(z, 2)
    d = 1 - 2 * hi
    m = lax.rem(z + hi, 2)
    edge, mid = m == 0, m == 1
    own = 2 * z + y

    def dev(zz, yy, cc):
        return 4 * zz + 2 * yy + cc

    sib, ydev = dev(z, y, 1 - c), dev(z, 1 - y, c)
    indev, outdev = dev(z + d, y, c), dev(z - d, y, c)

    def copy(src, p, s, target, sem):
        return pltpu.make_async_remote_copy(
            src_ref=src, dst_ref=G.at[p, c, s], send_sem=sem, recv_sem=recv.at[2 * p + c, s],
            device_id={"cols": target}, device_id_type=MESH)

    def await_chunk(p, cc, s):
        pltpu.make_async_remote_copy(
            src_ref=G.at[p, cc, s], dst_ref=G.at[p, cc, s], send_sem=s_sib.at[0, 0],
            recv_sem=recv.at[2 * p + cc, s], device_id={"cols": sib}, device_id_type=MESH).wait_recv()

    def mine(s):
        return og.at[:, pl.ds(s * width, width)]

    act_load = pltpu.make_async_copy(act, A, lsem.at[0])
    loads = [pltpu.make_async_copy(qry.at[q], Q.at[q], lsem.at[1 + q]) for q in range(2)]
    loads += [pltpu.make_async_copy(mine(s), G.at[own, c, s], lsem.at[3 + s]) for s in range(SUBS)]
    act_load.start()
    for load in loads:
        load.start()

    barrier = pltpu.get_barrier_semaphore()

    def greet(k, _):
        pl.semaphore_signal(barrier, inc=1, device_id={"cols": lax.rem(me + k, ncols)}, device_id_type=MESH)
        return 0

    lax.fori_loop(1, ncols, greet, 0)
    pl.semaphore_wait(barrier, ncols - 1)

    for s in range(SUBS):
        copy(mine(s), own, s, ydev, s_y.at[s]).start()
        copy(mine(s), own, s, indev, s_in.at[s]).start()

        @pl.when(mid)
        def _():
            copy(mine(s), own, s, outdev, s_out.at[s]).start()

        copy(mine(s), own, s, sib, s_sib.at[own, s]).start()

    acc[...] = jnp.zeros_like(acc)
    act_load.wait()

    def turn(p, _):
        total = jnp.zeros((8, 2 * tok), jnp.float32)
        for i in range(ff_dev // LANES):
            x = A[p, :, i * LANES:(i + 1) * LANES].astype(jnp.float32).T
            AT[p, i * LANES:(i + 1) * LANES, :] = x
            total = total + jnp.sum((x * x).reshape(LANES // 8, 8, 2 * tok), axis=0)
        asq[p] = total
        return 0

    lax.fori_loop(0, pairs, turn, 0)
    for load in loads:
        load.wait()

    row = lax.broadcasted_iota(jnp.int32, (8, 2 * tok), 0)
    qbase = jnp.zeros((8, 2 * tok), jnp.float32)
    for q in range(2):
        def add_squares(r, total):
            x = Q[q, pl.ds(pl.multiple_of(r * 16, 16), 16), :].astype(jnp.float32)
            x = x * x
            terms = [x[:, k * LANES:(k + 1) * LANES] for k in range(d_model // LANES)]
            while len(terms) > 1:
                terms = [a + b for a, b in zip(terms[::2], terms[1::2])]
            return total + terms[0]

        total = lax.fori_loop(0, ff_dev // 16, add_squares, jnp.zeros((16, LANES), jnp.float32))
        qbase = jnp.where(row == 3 + q, jnp.sum(total), qbase)
    qtile[...] = qbase
    x = jnp.zeros((tok, LANES), jnp.float32)
    for s in range(SUBS):
        for k in range(width // LANES):
            g = G[own, c, s, :, k * LANES:(k + 1) * LANES].astype(jnp.float32)
            x = x + g * g
    gsq[...] = x

    z1, zo = z + d, z - d
    other = 1 - y

    def inner_chunk(u):
        line = u < 12
        return (jnp.where(line, 2 * (z + d * (1 + lax.div(u, 4))) + y, 2 * z1 + other),
                jnp.where(line, lax.rem(u, 4), u - 10))

    def outer_chunk(u):
        line = u < 4
        return 2 * zo + jnp.where(line, y, other), jnp.where(line, u, u - 2)

    def y_chunk(u):
        ne = jnp.where(u < 6, u - 4, u - 2)
        from_out = jnp.logical_and(u < 8, lax.rem(u, 2) == 1)
        nm = jnp.where(u < 8, lax.div(u - 4, 2), u - 6)
        n = jnp.where(edge, ne, nm)
        zz = jnp.where(jnp.logical_and(mid, from_out), zo, z + d * (1 + lax.div(n, 4)))
        first = u < 4
        return (2 * jnp.where(first, z, zz) + other,
                jnp.where(first, u, lax.rem(n, 4)))

    def has_inner(u):
        return jnp.logical_and(u < 14, jnp.logical_or(edge, u < 8))

    def has_outer(u):
        return jnp.logical_and(mid, u < 6)

    def finish(p):
        tile = qtile[...]
        for k, value in enumerate((acc[p, 0], acc[p, 1], asq[p])):
            tile = jnp.where(row == k, jnp.sum(value, axis=0, keepdims=True), tile)
        for cc in range(2):
            target = 2 * p + cc
            half = tile[:, cc * tok:(cc + 1) * tok]
            res[p, cc] = half

            @pl.when(target == me)
            def _():
                parts[me] = half

            @pl.when(target != me)
            def _():
                pltpu.make_async_remote_copy(
                    src_ref=res.at[p, cc], dst_ref=parts.at[me], send_sem=r_send.at[p, cc],
                    recv_sem=r_recv.at[me], device_id={"cols": target}, device_id_type=MESH).start()

    def multiply(p, s_first, count, last):
        def one(j, _):
            s, q = s_first + lax.div(j, 2), lax.rem(j, 2)

            @pl.when(q == 0)
            def _():
                await_chunk(p, 1 - c, s)

            rhs = G[p, :, s].reshape(2 * tok, width)
            lhs = Q[q, :, pl.ds(pl.multiple_of(s * width, width), width)]
            pr = lax.dot_general(lhs, rhs, (((1,), (1,)), ((), ())), preferred_element_type=jnp.float32)
            acc[p, q] += jnp.sum((pr * AT[p]).reshape(ff_dev // 8, 8, 2 * tok), axis=0)
            return 0

        lax.fori_loop(0, 2 * count, one, 0)

        @pl.when(last)
        def _():
            finish(p)

    def step(u, _):
        def task(t, _):
            v = u - 1
            pi, si = inner_chunk(v)
            po, so = outer_chunk(v)
            py, sy = y_chunk(v)
            start = u == 0
            p = jnp.where(start, own, jnp.where(t == 0, pi, jnp.where(t == 1, po, py)))
            s = jnp.where(start, 0, jnp.where(t == 0, si, jnp.where(t == 1, so, sy)))
            go = jnp.where(t == 0, jnp.logical_or(start, has_inner(v)).astype(jnp.int32),
                           jnp.where(t == 1, jnp.logical_and(u > 0, has_outer(v)).astype(jnp.int32),
                                     (u > 0).astype(jnp.int32)))
            last_in = jnp.logical_or(start, si == 3)
            last_y = jnp.logical_or(sy == 3, jnp.logical_and(mid, v == 7))
            last = jnp.where(t == 0, last_in.astype(jnp.int32),
                             jnp.where(t == 1, (v == 3).astype(jnp.int32), last_y.astype(jnp.int32)))

            @pl.when(go == 1)
            def _():
                multiply(p, s, jnp.where(start, SUBS, 1), last == 1)

            return 0

        lax.fori_loop(0, 3, task, 0)

        @pl.when(has_inner(u))
        def _():
            p, s = inner_chunk(u)
            await_chunk(p, c, s)

            @pl.when(mid)
            def _():
                copy(G.at[p, c, s], p, s, outdev, s_out.at[4 + u]).start()

            skip = jnp.logical_and(edge, jnp.logical_or(jnp.logical_or(u == 2, u == 3), u >= 12))

            @pl.when(jnp.logical_not(skip))
            def _():
                k = jnp.where(edge, jnp.where(u < 2, 4 + u, u + 2), jnp.where(u < 2, 4 + 2 * u, u + 6))
                copy(G.at[p, c, s], p, s, ydev, s_y.at[k]).start()

            copy(G.at[p, c, s], p, s, sib, s_sib.at[p, s]).start()

        @pl.when(has_outer(u))
        def _():
            p, s = outer_chunk(u)
            await_chunk(p, c, s)

            @pl.when(u < 4)
            def _():
                copy(G.at[p, c, s], p, s, indev, s_in.at[4 + u]).start()

            @pl.when(u < 2)
            def _():
                copy(G.at[p, c, s], p, s, ydev, s_y.at[5 + 2 * u]).start()

            copy(G.at[p, c, s], p, s, sib, s_sib.at[p, s]).start()

        @pl.when(u < 14)
        def _():
            p, s = y_chunk(u)
            await_chunk(p, c, s)
            copy(G.at[p, c, s], p, s, sib, s_sib.at[p, s]).start()

            @pl.when(jnp.logical_and(edge, jnp.logical_or(u == 2, u == 3)))
            def _():
                copy(G.at[p, c, s], p, s, indev, s_in.at[2 + u]).start()

        @pl.when(jnp.logical_and(mid, jnp.logical_or(u == 8, u == 9)))
        def _():
            p, s = 2 * z + other, u - 6
            copy(G.at[p, c, s], p, s, outdev, s_out.at[4 + u]).start()

        return 0

    lax.fori_loop(0, 15, step, 0)

    def settle(sem):
        copy(mine(0), own, 0, sib, sem).wait_send()

    def settle_links(k, _):
        settle(s_y.at[k])

        @pl.when(mid)
        def _():
            settle(s_out.at[k])

        @pl.when(k < jnp.where(edge, 6, 8))
        def _():
            settle(s_in.at[k])

        return 0

    lax.fori_loop(0, 14, settle_links, 0)

    def settle_sib(p, _):
        for s in range(SUBS):
            settle(s_sib.at[p, s])
        return 0

    lax.fori_loop(0, pairs, settle_sib, 0)

    def gather_results(k, _):
        src = lax.rem(me + k, ncols)
        p, cc = lax.div(src, 2), lax.rem(src, 2)
        result = pltpu.make_async_remote_copy(
            src_ref=res.at[p, cc], dst_ref=parts.at[src], send_sem=r_send.at[p, cc],
            recv_sem=r_recv.at[src], device_id={"cols": src}, device_id_type=MESH)
        result.wait_recv()
        result.wait_send()
        return 0

    lax.fori_loop(1, ncols, gather_results, 0)

    full = parts[0]
    for src in range(1, ncols):
        full = full + parts[src]
    lane = lax.broadcasted_iota(jnp.int32, (1, tok), 1)
    query_rms = jnp.sqrt(full[3:5] / (ff * d_model) + epsilon)
    act_rms = jnp.sqrt(full[2:3] / ff + epsilon)
    grad_rms = jnp.sqrt(jnp.sum(gsq[...].T, axis=0, keepdims=True) / d_model + epsilon)
    positions = me * tok + lane
    seq_ids = lax.div(positions, LEN)
    limit = jnp.zeros((1, tok), jnp.int32)
    for q in range(seqs):
        limit = jnp.where(seq_ids == q, lens[q], limit)
    keep = lax.rem(positions, LEN) < limit
    influence = full[0:2] / (query_rms * act_rms * grad_rms * math.sqrt(ff * d_model))
    out[...] = jnp.where(keep, influence, 0.0)


def fused(ncols, activations, out_grads, queries, lengths):
    tok, d_model = out_grads.shape
    nq, ff_dev, _ = queries.shape
    pairs = ncols // 2
    sizes = (ncols, ff_dev * ncols, d_model, lengths.shape[0])
    tokens = ncols * tok
    dma = pltpu.SemaphoreType.DMA
    return pl.pallas_call(
        functools.partial(kernel, sizes),
        out_shape=jax.ShapeDtypeStruct((nq, tok), jnp.float32),
        in_specs=[pl.BlockSpec(memory_space=pl.ANY)] * 3 + [pl.BlockSpec(memory_space=pltpu.SMEM)],
        out_specs=pl.BlockSpec(memory_space=pltpu.VMEM),
        scratch_shapes=[
            pltpu.VMEM((pairs, 2, SUBS, tok, d_model // SUBS), jnp.bfloat16),
            pltpu.VMEM((pairs, 2 * tok, ff_dev), jnp.bfloat16),
            pltpu.VMEM((pairs, ff_dev, 2 * tok), jnp.float32),
            pltpu.VMEM((nq, ff_dev, d_model), jnp.bfloat16),
            pltpu.VMEM((pairs, nq, 8, 2 * tok), jnp.float32),
            pltpu.VMEM((pairs, 8, 2 * tok), jnp.float32),
            pltpu.VMEM((8, 2 * tok), jnp.float32),
            pltpu.VMEM((tok, LANES), jnp.float32),
            pltpu.VMEM((pairs, 2, 8, tok), jnp.float32),
            pltpu.VMEM((ncols, 8, tok), jnp.float32),
            dma((ncols, SUBS)), dma((8,)), dma((14,)), dma((14,)), dma((pairs, SUBS)),
            dma((pairs, 2)), dma((ncols,)), dma((3 + SUBS,)),
        ],
        compiler_params=pltpu.CompilerParams(
            collective_id=0, has_side_effects=True, vmem_limit_bytes=54 * 2**20),
        cost_estimate=pl.CostEstimate(
            flops=2 * nq * tokens * ff_dev * d_model, transcendentals=0,
            bytes_accessed=2 * (nq * ff_dev * d_model + tokens * ff_dev + tok * d_model)),
    )(out_grads, activations.reshape(pairs, 2 * tok, ff_dev), queries, lengths)


def local(activations, out_grads, queries, lengths):
    tok_dev, d_model = out_grads.shape
    query_sq = jnp.sum(jnp.square(queries.astype(jnp.float32)), axis=(1, 2))
    gathered = lax.all_gather(out_grads, "cols", axis=0, tiled=True)
    projected = jnp.einsum("rd,qfd->qrf", gathered, queries, preferred_element_type=jnp.float32)
    partials = jnp.sum(projected * activations.astype(jnp.float32)[None], axis=2)
    act_sq = jnp.sum(jnp.square(activations.astype(jnp.float32)), axis=1)[None, :]
    own_first = lax.axis_index("cols") * tok_dev
    total_scores, total_act, query_total = lax.psum((partials, act_sq, query_sq), "cols")
    own_scores = lax.dynamic_slice_in_dim(total_scores, own_first, tok_dev, 1)
    own_act = lax.dynamic_slice_in_dim(total_act, own_first, tok_dev, 1)
    ff = queries.shape[1] * lax.axis_size("cols")
    query_rms = jnp.sqrt(query_total / (ff * d_model) + epsilon)
    act_rms = jnp.sqrt(own_act[0] / ff + epsilon)
    grad_rms = jnp.sqrt(jnp.sum(jnp.square(out_grads.astype(jnp.float32)), axis=1) / d_model + epsilon)
    positions = own_first + jnp.arange(tok_dev, dtype=jnp.int32)
    seq_ids = positions // LEN
    owner_match = seq_ids[:, None] == jnp.arange(lengths.shape[0], dtype=jnp.int32)[None, :]
    seq_limit = jnp.sum(jnp.where(owner_match, lengths[None, :], 0), axis=1)
    keep_mask = positions % LEN < seq_limit
    denominator = query_rms[:, None] * act_rms[None, :] * grad_rms[None, :] * math.sqrt(ff * d_model)
    return jnp.where(keep_mask[None, :], own_scores / denominator, jnp.float32(0.0))


def solution(mesh):
    in_specs = (
        P("parts", "cols"),
        P(("parts", "cols"), None),
        P("parts", "cols", None),
        P("parts"),
    )
    out_specs = P(None, ("parts", "cols"))
    ncols = mesh.shape["cols"]
    body = functools.partial(fused, ncols) if ncols == 16 else local
    return jax.shard_map(body, mesh=mesh, in_specs=in_specs, out_specs=out_specs, check_vma=False)
```

```python
import functools
import math

import jax
import jax.numpy as jnp
from jax import lax
from jax.experimental import pallas as pl
from jax.experimental.pallas import tpu as pltpu
from jax.sharding import PartitionSpec as P

LEN = 1024
SUBS = 4
LANES = 128
MESH = pl.DeviceIdType.MESH

epsilon = 1e-06


def kernel(sizes, og, act, qry, lens, out, G, A, AT, Q, acc, asq, qtile, gsq, res, parts,
           recv, s_in, s_out, s_y, s_sib, r_send, r_recv, lsem):
    ncols, ff, d_model, seqs = sizes
    tok = og.shape[0]
    width = d_model // SUBS
    ff_dev = Q.shape[1]
    pairs = ncols // 2
    me = lax.axis_index("cols")
    z, y, c = lax.div(me, 4), lax.rem(lax.div(me, 2), 2), lax.rem(me, 2)
    hi = lax.div(z, 2)
    d = 1 - 2 * hi
    m = lax.rem(z + hi, 2)
    edge, mid = m == 0, m == 1
    own = 2 * z + y

    def dev(zz, yy, cc):
        return 4 * zz + 2 * yy + cc

    sib, ydev = dev(z, y, 1 - c), dev(z, 1 - y, c)
    indev, outdev = dev(z + d, y, c), dev(z - d, y, c)

    def copy(src, p, s, target, sem):
        return pltpu.make_async_remote_copy(
            src_ref=src, dst_ref=G.at[p, c, s], send_sem=sem, recv_sem=recv.at[2 * p + c, s],
            device_id={"cols": target}, device_id_type=MESH)

    def await_chunk(p, cc, s):
        pltpu.make_async_remote_copy(
            src_ref=G.at[p, cc, s], dst_ref=G.at[p, cc, s], send_sem=s_sib.at[0, 0],
            recv_sem=recv.at[2 * p + cc, s], device_id={"cols": sib}, device_id_type=MESH).wait_recv()

    def mine(s):
        return og.at[:, pl.ds(s * width, width)]

    act_load = pltpu.make_async_copy(act, A, lsem.at[0])
    loads = [pltpu.make_async_copy(qry.at[q], Q.at[q], lsem.at[1 + q]) for q in range(2)]
    loads += [pltpu.make_async_copy(mine(s), G.at[own, c, s], lsem.at[3 + s]) for s in range(SUBS)]
    act_load.start()
    for load in loads:
        load.start()

    barrier = pltpu.get_barrier_semaphore()

    def greet(target):
        pl.semaphore_signal(barrier, inc=1, device_id={"cols": target}, device_id_type=MESH)

    for target in (sib, ydev, indev):
        greet(target)

    @pl.when(mid)
    def _():
        greet(outdev)

    pl.semaphore_wait(barrier, 3 + m)

    for s in range(SUBS):
        copy(mine(s), own, s, ydev, s_y.at[s]).start()
        copy(mine(s), own, s, indev, s_in.at[s]).start()

        @pl.when(mid)
        def _():
            copy(mine(s), own, s, outdev, s_out.at[s]).start()

        copy(mine(s), own, s, sib, s_sib.at[own, s]).start()

    acc[...] = jnp.zeros_like(acc)
    act_load.wait()

    def turn(p, _):
        total = jnp.zeros((8, 2 * tok), jnp.float32)
        for i in range(ff_dev // LANES):
            x = A[p, :, i * LANES:(i + 1) * LANES].astype(jnp.float32).T
            AT[p, i * LANES:(i + 1) * LANES, :] = x
            total = total + jnp.sum((x * x).reshape(LANES // 8, 8, 2 * tok), axis=0)
        asq[p] = total
        return 0

    lax.fori_loop(0, pairs, turn, 0)
    for load in loads:
        load.wait()

    row = lax.broadcasted_iota(jnp.int32, (8, 2 * tok), 0)
    qbase = jnp.zeros((8, 2 * tok), jnp.float32)
    for q in range(2):
        def add_squares(r, total):
            x = Q[q, pl.ds(pl.multiple_of(r * 16, 16), 16), :].astype(jnp.float32)
            x = x * x
            terms = [x[:, k * LANES:(k + 1) * LANES] for k in range(d_model // LANES)]
            while len(terms) > 1:
                terms = [a + b for a, b in zip(terms[::2], terms[1::2])]
            return total + terms[0]

        total = lax.fori_loop(0, ff_dev // 16, add_squares, jnp.zeros((16, LANES), jnp.float32))
        qbase = jnp.where(row == 3 + q, jnp.sum(total), qbase)
    qtile[...] = qbase
    x = jnp.zeros((tok, LANES), jnp.float32)
    for s in range(SUBS):
        for k in range(width // LANES):
            g = G[own, c, s, :, k * LANES:(k + 1) * LANES].astype(jnp.float32)
            x = x + g * g
    gsq[...] = x

    z1, zo = z + d, z - d
    other = 1 - y

    def inner_chunk(u):
        line = u < 12
        return (jnp.where(line, 2 * (z + d * (1 + lax.div(u, 4))) + y, 2 * z1 + other),
                jnp.where(line, lax.rem(u, 4), u - 10))

    def outer_chunk(u):
        line = u < 4
        return 2 * zo + jnp.where(line, y, other), jnp.where(line, u, u - 2)

    def y_chunk(u):
        ne = jnp.where(u < 6, u - 4, u - 2)
        from_out = jnp.logical_and(u < 8, lax.rem(u, 2) == 1)
        nm = jnp.where(u < 8, lax.div(u - 4, 2), u - 6)
        n = jnp.where(edge, ne, nm)
        zz = jnp.where(jnp.logical_and(mid, from_out), zo, z + d * (1 + lax.div(n, 4)))
        first = u < 4
        return (2 * jnp.where(first, z, zz) + other,
                jnp.where(first, u, lax.rem(n, 4)))

    def has_inner(u):
        return jnp.logical_and(u < 14, jnp.logical_or(edge, u < 8))

    def has_outer(u):
        return jnp.logical_and(mid, u < 6)

    def settle(sem):
        copy(mine(0), own, 0, sib, sem).wait_send()

    def settle_links(k, _):
        settle(s_y.at[k])

        @pl.when(mid)
        def _():
            settle(s_out.at[k])

        @pl.when(k < jnp.where(edge, 6, 8))
        def _():
            settle(s_in.at[k])

        return 0

    def finish(p):
        tile = qtile[...]
        for k, value in enumerate((acc[p, 0], acc[p, 1], asq[p])):
            tile = jnp.where(row == k, jnp.sum(value, axis=0, keepdims=True), tile)
        for cc in range(2):
            target = 2 * p + cc
            half = tile[:, cc * tok:(cc + 1) * tok]
            res[p, cc] = half

            @pl.when(target == me)
            def _():
                parts[me] = half

            @pl.when(target != me)
            def _():
                pltpu.make_async_remote_copy(
                    src_ref=res.at[p, cc], dst_ref=parts.at[me], send_sem=r_send.at[p, cc],
                    recv_sem=r_recv.at[me], device_id={"cols": target}, device_id_type=MESH).start()

    def multiply(p, s_first, count, last):
        def one(j, _):
            s, q = s_first + lax.div(j, 2), lax.rem(j, 2)

            @pl.when(q == 0)
            def _():
                await_chunk(p, 1 - c, s)

            rhs = G[p, :, s].reshape(2 * tok, width)
            lhs = Q[q, :, pl.ds(pl.multiple_of(s * width, width), width)]
            pr = lax.dot_general(lhs, rhs, (((1,), (1,)), ((), ())), preferred_element_type=jnp.float32)
            acc[p, q] += jnp.sum((pr * AT[p]).reshape(ff_dev // 8, 8, 2 * tok), axis=0)

            @pl.when(q == 1)
            def _():
                settle(s_sib.at[p, s])

            return 0

        lax.fori_loop(0, 2 * count, one, 0)

        @pl.when(last)
        def _():
            finish(p)

    def step(u, _):
        def task(t, _):
            v = u - 1
            pi, si = inner_chunk(v)
            po, so = outer_chunk(v)
            py, sy = y_chunk(v)
            start = u == 0
            p = jnp.where(start, own, jnp.where(t == 0, pi, jnp.where(t == 1, po, py)))
            s = jnp.where(start, 0, jnp.where(t == 0, si, jnp.where(t == 1, so, sy)))
            go = jnp.where(t == 0, jnp.logical_or(start, has_inner(v)).astype(jnp.int32),
                           jnp.where(t == 1, jnp.logical_and(u > 0, has_outer(v)).astype(jnp.int32),
                                     (u > 0).astype(jnp.int32)))
            last_in = jnp.logical_or(start, si == 3)
            last_y = jnp.logical_or(sy == 3, jnp.logical_and(mid, v == 7))
            last = jnp.where(t == 0, last_in.astype(jnp.int32),
                             jnp.where(t == 1, (v == 3).astype(jnp.int32), last_y.astype(jnp.int32)))

            @pl.when(go == 1)
            def _():
                multiply(p, s, jnp.where(start, SUBS, 1), last == 1)

            return 0

        lax.fori_loop(0, 3, task, 0)

        @pl.when(jnp.logical_and(u >= 4, u < 14))
        def _():
            settle_links(u - 4, 0)

        @pl.when(has_inner(u))
        def _():
            p, s = inner_chunk(u)
            await_chunk(p, c, s)

            @pl.when(mid)
            def _():
                copy(G.at[p, c, s], p, s, outdev, s_out.at[4 + u]).start()

            skip = jnp.logical_and(edge, jnp.logical_or(jnp.logical_or(u == 2, u == 3), u >= 12))

            @pl.when(jnp.logical_not(skip))
            def _():
                k = jnp.where(edge, jnp.where(u < 2, 4 + u, u + 2), jnp.where(u < 2, 4 + 2 * u, u + 6))
                copy(G.at[p, c, s], p, s, ydev, s_y.at[k]).start()

            copy(G.at[p, c, s], p, s, sib, s_sib.at[p, s]).start()

        @pl.when(has_outer(u))
        def _():
            p, s = outer_chunk(u)
            await_chunk(p, c, s)

            @pl.when(u < 4)
            def _():
                copy(G.at[p, c, s], p, s, indev, s_in.at[4 + u]).start()

            @pl.when(u < 2)
            def _():
                copy(G.at[p, c, s], p, s, ydev, s_y.at[5 + 2 * u]).start()

            copy(G.at[p, c, s], p, s, sib, s_sib.at[p, s]).start()

        @pl.when(u < 14)
        def _():
            p, s = y_chunk(u)
            await_chunk(p, c, s)
            copy(G.at[p, c, s], p, s, sib, s_sib.at[p, s]).start()

            @pl.when(jnp.logical_and(edge, jnp.logical_or(u == 2, u == 3)))
            def _():
                copy(G.at[p, c, s], p, s, indev, s_in.at[2 + u]).start()

        @pl.when(jnp.logical_and(mid, jnp.logical_or(u == 8, u == 9)))
        def _():
            p, s = 2 * z + other, u - 6
            copy(G.at[p, c, s], p, s, outdev, s_out.at[4 + u]).start()

        return 0

    lax.fori_loop(0, 15, step, 0)

    lax.fori_loop(10, 14, settle_links, 0)

    def gather_results(k, _):
        src = lax.rem(me + k, ncols)
        p, cc = lax.div(src, 2), lax.rem(src, 2)
        result = pltpu.make_async_remote_copy(
            src_ref=res.at[p, cc], dst_ref=parts.at[src], send_sem=r_send.at[p, cc],
            recv_sem=r_recv.at[src], device_id={"cols": src}, device_id_type=MESH)
        result.wait_recv()
        result.wait_send()
        return 0

    lax.fori_loop(1, ncols, gather_results, 0)

    full = parts[0]
    for src in range(1, ncols):
        full = full + parts[src]
    lane = lax.broadcasted_iota(jnp.int32, (1, tok), 1)
    query_rms = jnp.sqrt(full[3:5] / (ff * d_model) + epsilon)
    act_rms = jnp.sqrt(full[2:3] / ff + epsilon)
    grad_rms = jnp.sqrt(jnp.sum(gsq[...].T, axis=0, keepdims=True) / d_model + epsilon)
    positions = me * tok + lane
    seq_ids = lax.div(positions, LEN)
    limit = jnp.zeros((1, tok), jnp.int32)
    for q in range(seqs):
        limit = jnp.where(seq_ids == q, lens[q], limit)
    keep = lax.rem(positions, LEN) < limit
    influence = full[0:2] / (query_rms * act_rms * grad_rms * math.sqrt(ff * d_model))
    out[...] = jnp.where(keep, influence, 0.0)


def fused(ncols, activations, out_grads, queries, lengths):
    tok, d_model = out_grads.shape
    nq, ff_dev, _ = queries.shape
    pairs = ncols // 2
    sizes = (ncols, ff_dev * ncols, d_model, lengths.shape[0])
    tokens = ncols * tok
    dma = pltpu.SemaphoreType.DMA
    return pl.pallas_call(
        functools.partial(kernel, sizes),
        out_shape=jax.ShapeDtypeStruct((nq, tok), jnp.float32),
        in_specs=[pl.BlockSpec(memory_space=pl.ANY)] * 3 + [pl.BlockSpec(memory_space=pltpu.SMEM)],
        out_specs=pl.BlockSpec(memory_space=pltpu.VMEM),
        scratch_shapes=[
            pltpu.VMEM((pairs, 2, SUBS, tok, d_model // SUBS), jnp.bfloat16),
            pltpu.VMEM((pairs, 2 * tok, ff_dev), jnp.bfloat16),
            pltpu.VMEM((pairs, ff_dev, 2 * tok), jnp.float32),
            pltpu.VMEM((nq, ff_dev, d_model), jnp.bfloat16),
            pltpu.VMEM((pairs, nq, 8, 2 * tok), jnp.float32),
            pltpu.VMEM((pairs, 8, 2 * tok), jnp.float32),
            pltpu.VMEM((8, 2 * tok), jnp.float32),
            pltpu.VMEM((tok, LANES), jnp.float32),
            pltpu.VMEM((pairs, 2, 8, tok), jnp.float32),
            pltpu.VMEM((ncols, 8, tok), jnp.float32),
            dma((ncols, SUBS)), dma((8,)), dma((14,)), dma((14,)), dma((pairs, SUBS)),
            dma((pairs, 2)), dma((ncols,)), dma((3 + SUBS,)),
        ],
        compiler_params=pltpu.CompilerParams(
            collective_id=0, has_side_effects=True, vmem_limit_bytes=54 * 2**20),
        cost_estimate=pl.CostEstimate(
            flops=2 * nq * tokens * ff_dev * d_model, transcendentals=0,
            bytes_accessed=2 * (nq * ff_dev * d_model + tokens * ff_dev + tok * d_model)),
    )(out_grads, activations.reshape(pairs, 2 * tok, ff_dev), queries, lengths)


def local(activations, out_grads, queries, lengths):
    tok_dev, d_model = out_grads.shape
    query_sq = jnp.sum(jnp.square(queries.astype(jnp.float32)), axis=(1, 2))
    gathered = lax.all_gather(out_grads, "cols", axis=0, tiled=True)
    projected = jnp.einsum("rd,qfd->qrf", gathered, queries, preferred_element_type=jnp.float32)
    partials = jnp.sum(projected * activations.astype(jnp.float32)[None], axis=2)
    act_sq = jnp.sum(jnp.square(activations.astype(jnp.float32)), axis=1)[None, :]
    own_first = lax.axis_index("cols") * tok_dev
    total_scores, total_act, query_total = lax.psum((partials, act_sq, query_sq), "cols")
    own_scores = lax.dynamic_slice_in_dim(total_scores, own_first, tok_dev, 1)
    own_act = lax.dynamic_slice_in_dim(total_act, own_first, tok_dev, 1)
    ff = queries.shape[1] * lax.axis_size("cols")
    query_rms = jnp.sqrt(query_total / (ff * d_model) + epsilon)
    act_rms = jnp.sqrt(own_act[0] / ff + epsilon)
    grad_rms = jnp.sqrt(jnp.sum(jnp.square(out_grads.astype(jnp.float32)), axis=1) / d_model + epsilon)
    positions = own_first + jnp.arange(tok_dev, dtype=jnp.int32)
    seq_ids = positions // LEN
    owner_match = seq_ids[:, None] == jnp.arange(lengths.shape[0], dtype=jnp.int32)[None, :]
    seq_limit = jnp.sum(jnp.where(owner_match, lengths[None, :], 0), axis=1)
    keep_mask = positions % LEN < seq_limit
    denominator = query_rms[:, None] * act_rms[None, :] * grad_rms[None, :] * math.sqrt(ff * d_model)
    return jnp.where(keep_mask[None, :], own_scores / denominator, jnp.float32(0.0))


def solution(mesh):
    in_specs = (
        P("parts", "cols"),
        P(("parts", "cols"), None),
        P("parts", "cols", None),
        P("parts"),
    )
    out_specs = P(None, ("parts", "cols"))
    ncols = mesh.shape["cols"]
    body = functools.partial(fused, ncols) if ncols == 16 else local
    return jax.shard_map(body, mesh=mesh, in_specs=in_specs, out_specs=out_specs, check_vma=False)
```
